32 devices in a mesh: rec: 4 (over z), tm: 8 (over y, x, core).
Axes of the slice: x: 2, y: 2, z: 4, core: 2. Of those that a mesh axis runs over, the one named last changes fastest.
Arguments:
- audio: float32 [4, 40960], P('rec', 'tm'), may hold values from -100 to 100, as said below
- conv0_weight: float32 [10, 512], replicated, may hold values from -2 to 2
- norm_gain: float32 [512], replicated, may hold values from 0.25 to 1.75
- norm_bias: float32 [512], replicated, may hold values from -3 to 3
- conv1_weight: bfloat16 [1536, 512], replicated, may hold values from -0.25 to 0.25
- conv2_weight: bfloat16 [1536, 512], replicated, may hold values from -0.25 to 0.25
- cotangent: bfloat16 [4, 2048, 512], P('rec', 'tm'), may hold values from -0.09375 to 0.09375
Outputs:
- features: bfloat16 [4, 2048, 512], P('rec', 'tm')
- grad_conv0: float32 [10, 512], replicated
- grad_gain: float32 [512], replicated
- grad_bias: float32 [512], replicated
- grad_conv1: float32 [1536, 512], replicated
- grad_conv2: float32 [1536, 512], replicated
The draws below stay inside these ranges and needn't reach their ends.
Inputs may be any that keep to these rules, and one draw needn't show every extreme that they name: `audio`: recorded waveforms, one row a recording.
All inputs are finite; a program needn't handle non-finite values.
Results may differ from the reference program's by a relative error of at most 0.0095.
Values may be sent and summed in bfloat16 or wider, within the bound.
A program may use at most 64 MiB of HBM per device.

```python
import math
import jax
import jax.numpy as jnp
from jax import lax

C = 512
FRAMES_DEV = 256
RECS = 4
FRAMES = 2048
SAMPLES = 40960


def draw_audio(key, part):
    noise_key = jax.random.fold_in(key, 11)
    level_key = jax.random.fold_in(key, 23)
    piece_key = jax.random.fold_in(key, 37)
    span = 20 * FRAMES_DEV
    pieces = SAMPLES // span
    position = jnp.arange(SAMPLES, dtype=jnp.float32) / (SAMPLES * 1.0)
    level = jnp.exp(jax.random.uniform(level_key, (RECS, 1), jnp.float32, math.log(0.5), math.log(2.0)))
    piece_level = jnp.exp(jax.random.uniform(piece_key, (RECS, pieces, 1), jnp.float32, math.log(0.25), math.log(4.0)))
    rough = jnp.broadcast_to(piece_level, (RECS, pieces, span)).reshape(RECS, SAMPLES)
    noise = jnp.clip(jax.random.normal(noise_key, (RECS, SAMPLES), jnp.float32), -4.0, 4.0)
    envelope = 3.0 * jnp.exp(position * -math.log(3.0))
    return jnp.clip(noise * envelope[None, :] * level * rough, -100.0, 100.0)


def strengthened(values, key, source, target, shards_of, factor):
    def block_of(dim):
        return (jnp.arange(values.shape[dim]) // (values.shape[dim] // shards_of)).reshape((-1,) + (1,) * (values.ndim - 1 - dim))

    first = jax.random.permutation(key, shards_of)[block_of(target)]
    other_side = (block_of(target) + shards_of // 2) % shards_of
    return jnp.where((block_of(source) == first) | (block_of(source) == other_side), factor * values, values)


def levels(own_key, dims, shards, least, high):
    loudness, own = 1.0, jax.random.fold_in(own_key, 6)
    for dim, shards_of in shards:
        steps = jnp.exp(jax.random.uniform(jax.random.fold_in(own, dim), (shards_of,), jnp.float32, least / len(shards), high / len(shards)))
        loudness = loudness * jnp.repeat(steps, dims[dim] // shards_of).reshape([-1 if axis == dim else 1 for axis in range(len(dims))])
    return loudness


def bell_draw(rng, dims, width, bound, shards=(), kind=jnp.bfloat16):
    drawn = jax.random.normal(rng, dims, jnp.float32) * width
    if len(shards) > 0:
        drawn = levels(rng, dims, shards, -0.22, 0.18) * drawn
    return jnp.clip(drawn, min=-bound, max=bound).astype(kind)


def gaussian_with(own_key, dims, spread, limit, split, heavy, held_as=jnp.bfloat16):
    drawn = spread * jax.random.normal(own_key, dims, jnp.float32)
    if split:
        drawn = drawn * levels(own_key, dims, split, -0.22, 0.18)
    return jnp.clip(strengthened(drawn, jax.random.fold_in(own_key, 3), *heavy), -limit, limit).astype(held_as)


def setup_inputs(seed: int = 0) -> dict:
    arg_keys = jax.random.split(jax.random.key(seed), 8)
    return {
        "audio": draw_audio(jax.random.fold_in(arg_keys[7], 71), 0),
        "conv0_weight": bell_draw(arg_keys[1], (10, C), 10 ** -0.5, 2.0, (), jnp.float32),
        "norm_gain": jnp.clip(1.0 + 0.15 * jax.random.normal(arg_keys[2], (C,), jnp.float32), 0.25, 1.75),
        "norm_bias": bell_draw(arg_keys[3], (C,), 0.5, 3.0, (), jnp.float32),
        "conv1_weight": bell_draw(arg_keys[4], (3 * C, C), C ** -0.5, 0.25),
        "conv2_weight": bell_draw(arg_keys[5], (3 * C, C), C ** -0.5, 0.25),
        "cotangent": gaussian_with(arg_keys[6], (RECS, FRAMES, C), ((FRAMES * RECS) ** -0.5), 0.09375, ((0, 4), (1, 8)), (1, 2, 8, 2.0)),
    }


EPS = 1e-05
HIGH = lax.Precision.HIGHEST

def gelu_slope(value):
    return 0.5 * (1.0 + lax.erf(value * 0.7071067811865476)) + value * jnp.exp(-0.5 * value * value) * 0.3989422804014327

def stride_conv(active, weight):
    channels = active.shape[1]
    pairs = active.reshape(active.shape[0] // 2, 2 * channels)
    following = jnp.concatenate([pairs[1:, :channels], jnp.zeros((1, channels), active.dtype)], 0)
    output = jnp.dot(pairs, weight[:2 * channels], preferred_element_type=jnp.float32)
    output = output + jnp.dot(following, weight[2 * channels:], preferred_element_type=jnp.float32)
    return (pairs, following, output)

def weight_grad(pairs, following, delta):
    upper = jnp.dot(pairs.T, delta, preferred_element_type=jnp.float32)
    lower = jnp.dot(following.T, delta, preferred_element_type=jnp.float32)
    return jnp.concatenate([upper, lower], 0)

def stride_back(delta, weight):
    channels = delta.shape[1]
    before = jnp.concatenate([jnp.zeros((1, channels), delta.dtype), delta[:-1]], 0)
    back_pairs = jnp.dot(delta, weight[:2 * channels].T, preferred_element_type=jnp.float32)
    shifted = jnp.dot(before, weight[2 * channels:].T, preferred_element_type=jnp.float32)
    even_rows = back_pairs[:, :channels] + shifted
    return jnp.concatenate([even_rows, back_pairs[:, channels:]], 1).reshape(-1, channels)

def one_recording(samples, cotan, conv0_weight, norm_gain, norm_bias, conv1_weight, conv2_weight):
    blocks = samples.reshape(-1, 5)
    following = jnp.concatenate([blocks[1:], jnp.zeros((1, 5), blocks.dtype)], 0)
    patches = jnp.concatenate([blocks, following], 1)
    pre_norm = jnp.dot(patches, conv0_weight, precision=HIGH)
    count = pre_norm.shape[0] * 1.0
    mean = lax.optimization_barrier(jnp.sum(pre_norm, 0)) / count
    centered = pre_norm - mean
    variance = lax.optimization_barrier(jnp.sum(centered * centered, 0)) / count
    inverse = lax.rsqrt(variance + EPS)
    normed = centered * inverse
    shifted_norm = normed * norm_gain + norm_bias
    act0 = jax.nn.gelu(shifted_norm, approximate=False).astype(jnp.bfloat16)
    pairs1, follow1, pre1 = stride_conv(act0, conv1_weight)
    act1 = jax.nn.gelu(pre1, approximate=False).astype(jnp.bfloat16)
    pairs2, follow2, pre2 = stride_conv(act1, conv2_weight)
    features = jax.nn.gelu(pre2, approximate=False).astype(jnp.bfloat16)
    delta2 = (cotan.astype(jnp.float32) * gelu_slope(pre2)).astype(jnp.bfloat16)
    grad_two = weight_grad(pairs2, follow2, delta2)
    back1 = stride_back(delta2, conv2_weight)
    delta1 = (back1 * gelu_slope(pre1)).astype(jnp.bfloat16)
    grad_one = weight_grad(pairs1, follow1, delta1)
    back0 = stride_back(delta1, conv1_weight)
    dnorm = back0 * gelu_slope(shifted_norm)
    sum_one = lax.optimization_barrier(jnp.sum(dnorm, 0))
    sum_two = lax.optimization_barrier(jnp.sum(dnorm * normed, 0))
    scale = norm_gain * inverse
    dpre = scale * (dnorm - sum_one / count - normed * (sum_two / count))
    grad_zero = jnp.dot(patches.T, dpre, precision=HIGH)
    return (features, grad_zero, sum_two, sum_one, grad_one, grad_two)

def reference(audio, conv0_weight, norm_gain, norm_bias, conv1_weight, conv2_weight, cotangent):

    def step(pair):
        return one_recording(pair[0], pair[1], conv0_weight, norm_gain, norm_bias, conv1_weight, conv2_weight)
    outs = lax.map(step, (audio, cotangent))
    features = outs[0]
    grad_conv0 = lax.optimization_barrier(jnp.sum(outs[1], 0))
    grad_gain = lax.optimization_barrier(jnp.sum(outs[2], 0))
    grad_bias = lax.optimization_barrier(jnp.sum(outs[3], 0))
    grad_conv1 = lax.optimization_barrier(jnp.sum(outs[4], 0))
    grad_conv2 = lax.optimization_barrier(jnp.sum(outs[5], 0))
    return (features, grad_conv0, grad_gain, grad_bias, grad_conv1, grad_conv2)
```

```python
import functools

import jax
import jax.numpy as jnp
from jax import lax
from jax.experimental import pallas as pl
from jax.experimental.pallas import tpu as pltpu
from jax.sharding import PartitionSpec as P

EPS = 1e-05
HIGH = lax.Precision.HIGHEST
MESH = pl.DeviceIdType.MESH
F32, BF16 = jnp.float32, jnp.bfloat16
EDGE = 16
STEP = 16


def from_behind(value, axis, steps):
    count = lax.axis_size(axis)
    leading, last = (max(0, -steps), min(count, count - steps))
    return lax.ppermute(value, axis, [(source, source + steps) for source in range(leading, last)])


def gelu_parts(value):
    phi = 0.5 * (1.0 + lax.erf(value * 0.7071067811865476))
    slope = phi + value * jnp.exp(-0.5 * value * value) * 0.3989422804014327
    return value * phi, slope


def dot(a, b, ca, cb, precision=None):
    return lax.dot_general(
        a, b, (((ca,), (cb,)), ((), ())), precision=precision, preferred_element_type=F32
    )


def plan(tm, rec):
    inner = [("tm", 1 << i) for i in range(1, tm.bit_length() - 1)]
    low, high = inner[: len(inner) // 2], inner[len(inner) // 2 :]
    outer = [("rec", 1 << i) for i in range(rec.bit_length() - 1)]
    core = [("tm", 1)]
    return core, [core + low + high + outer, core + high + outer + low, core + outer + low + high]


def kernel(
    tm, rec, patches_ref, taps_ref, gain_ref, bias_ref, w1_ref, w2_ref, cot_ref,
    features_ref, res_ref, small_ref,
    norm_ref, slope0_ref, act0_ref, pre1_ref, slope1_ref, act1_ref, pre2_ref, delta2_ref, delta1_ref,
    dn_ref, t0_ref, t1_ref, gf_ref, sendbuf, recvbuf, stat_ref, stat_in, little, little_in,
    rs_send, rs_recv, st_send, st_recv, sm_send, sm_recv,
):
    me = {"tm": lax.axis_index("tm"), "rec": lax.axis_index("rec")}
    rows_all, channels = norm_ref.shape[0], gain_ref.shape[1]
    rows = rows_all - EDGE
    count = 4.0 * rows * tm
    _, orders = plan(tm, rec)
    third = gf_ref.shape[0] // 3
    C = channels

    def bit_of(stage):
        axis, bit = stage
        return lax.rem(me[axis] // bit, 2)

    def partner(stage):
        axis, bit = stage
        return {axis: me[axis] + bit * (1 - 2 * bit_of(stage))}

    barrier = pltpu.get_barrier_semaphore()
    rec_bits = [s for s in orders[0] if s[0] == "rec"]
    for d in range(1, tm):
        pl.semaphore_signal(barrier, inc=1, device_id={"tm": lax.rem(me["tm"] + d, tm)}, device_id_type=MESH)
    for stage in rec_bits:
        pl.semaphore_signal(barrier, inc=1, device_id=partner(stage), device_id_type=MESH)

    for q in range(4):
        norm_ref[:, q * C : (q + 1) * C] = dot(patches_ref[q], taps_ref[...], 1, 0, HIGH)

    def sums(i, carry):
        one, two = carry
        for q in range(4):
            part = norm_ref[pl.ds(i * STEP, STEP), q * C : (q + 1) * C]
            one, two = one + part, two + part * part
        return one, two

    zero = jnp.zeros((STEP, C), F32)
    one, two = lax.fori_loop(0, rows // STEP, sums, (zero, zero))
    stat_ref[0, 0:1, :] = jnp.sum(one, 0, keepdims=True)
    stat_ref[0, 1:2, :] = jnp.sum(two, 0, keepdims=True)
    pl.semaphore_wait(barrier, tm - 1 + len(rec_bits))

    def share(which):
        copies = []
        for d in range(1, tm):
            copy = pltpu.make_async_remote_copy(
                src_ref=stat_ref.at[which],
                dst_ref=stat_in.at[which, d],
                send_sem=st_send.at[which, d],
                recv_sem=st_recv.at[which, d],
                device_id={"tm": lax.rem(me["tm"] + d, tm)},
                device_id_type=MESH,
            )
            copy.start()
            copies.append(copy)
        return copies

    def gathered(which, copies):
        total = stat_ref[which]
        for d, copy in enumerate(copies):
            copy.wait_recv()
            total = total + stat_in[which, d + 1]
        for copy in copies:
            copy.wait_send()
        return total

    total = gathered(0, share(0))
    mean = total[0:1] / count
    variance = total[1:2] / count - mean * mean
    inverse = lax.rsqrt(variance + EPS)
    gain, bias = gain_ref[...], bias_ref[...]

    def first_act(i, carry):
        at = pl.ds(pl.multiple_of(i * STEP, STEP), STEP)
        row = i * STEP + lax.broadcasted_iota(jnp.int32, (STEP, C), 0)
        past = jnp.logical_and(row == rows, me["tm"] == tm - 1)
        for q in range(4):
            lanes = slice(q * C, (q + 1) * C)
            normed = (norm_ref[at, lanes] - mean) * inverse
            norm_ref[at, lanes] = normed
            act, slope = gelu_parts(normed * gain + bias)
            act0_ref[at, lanes] = jnp.where(past, 0.0, act).astype(BF16)
            slope0_ref[at, lanes] = slope
        return carry

    lax.fori_loop(0, rows_all // STEP, first_act, 0)
    act0_ref[:, 4 * C :] = pltpu.roll(act0_ref[:, :C].astype(F32), rows_all - 1, 0).astype(BF16)

    pre1_ref[:, :C] = dot(act0_ref[:, : 3 * C], w1_ref[...], 1, 0)
    pre1_ref[:, C:] = dot(act0_ref[:, 2 * C :], w1_ref[...], 1, 0)

    def second_act(i, carry):
        at = pl.ds(pl.multiple_of(i * STEP, STEP), STEP)
        row = i * STEP + lax.broadcasted_iota(jnp.int32, (STEP, 2 * C), 0)
        past = jnp.logical_and(row == rows, me["tm"] == tm - 1)
        act, slope = gelu_parts(pre1_ref[at, :])
        act1_ref[at, : 2 * C] = jnp.where(past, 0.0, act).astype(BF16)
        slope1_ref[at, :] = slope
        return carry

    lax.fori_loop(0, rows_all // STEP, second_act, 0)
    act1_ref[:, 2 * C :] = pltpu.roll(act1_ref[:, :C].astype(F32), rows_all - 1, 0).astype(BF16)

    pre2_ref[...] = dot(act1_ref[...], w2_ref[...], 1, 0)

    def third_act(i, carry):
        at = pl.ds(pl.multiple_of(i * STEP, STEP), STEP)
        act, slope = gelu_parts(pre2_ref[at, :])
        pre2_ref[at, :] = act
        delta2_ref[at, :] = (cot_ref[at, :].astype(F32) * slope).astype(BF16)
        return carry

    lax.fori_loop(0, rows_all // STEP, third_act, 0)
    features_ref[...] = pre2_ref[:rows, :].astype(BF16)

    state = [[third, part * third, 0, []] for part in range(3)]

    def narrow(ref, source, start, size):
        block = min(32, size)

        def body(i, carry):
            at = pl.ds(pl.multiple_of(start + i * block, block), block)
            ref[at, :] = source[at, :].astype(BF16)
            return carry

        lax.fori_loop(0, size // block, body, 0)

    def launch(part):
        size, start, used, sent = state[part]
        stage = orders[part][len(sent)]
        half = size // 2 if size // 2 >= 16 else size
        bit = bit_of(stage) if half < size else 0
        keep = start + bit * half
        away = start + (1 - bit) * half if half < size else start
        narrow(sendbuf, gf_ref, away, half)
        copy = pltpu.make_async_remote_copy(
            src_ref=sendbuf.at[pl.ds(pl.multiple_of(away, 16), half), :],
            dst_ref=recvbuf.at[part, pl.ds(used, half), :],
            send_sem=rs_send.at[part, len(sent)],
            recv_sem=rs_recv.at[part, len(sent)],
            device_id=partner(stage),
            device_id_type=MESH,
        )
        copy.start()
        sent.append((copy, keep, size, start, half))

    def absorb(part):
        size, start, used, sent = state[part]
        copy, keep, _, _, half = sent[-1]
        copy.wait_recv()
        if half == size:
            copy.wait_send()
        block = min(32, half)

        def body(i, carry):
            at = pl.ds(pl.multiple_of(keep + i * block, block), block)
            came = recvbuf[part, pl.ds(pl.multiple_of(used + i * block, 16), block), :]
            gf_ref[at, :] = gf_ref[at, :] + came.astype(F32)
            return carry

        lax.fori_loop(0, half // block, body, 0)
        state[part][0], state[part][1], state[part][2] = half, keep, used + half

    gf_ref[: 3 * C, :] = dot(act1_ref[:rows, :], delta2_ref[:rows, :], 0, 0)
    launch(0)
    t0_ref[...] = dot(delta2_ref[...], w2_ref[...], 1, 1)
    even = t0_ref[:, :C] + pltpu.roll(t0_ref[:, 2 * C :], 1, 0)
    delta1_ref[:, :C] = (even * slope1_ref[:, :C]).astype(BF16)
    delta1_ref[:, C:] = (t0_ref[:, C : 2 * C] * slope1_ref[:, C:]).astype(BF16)

    gf_ref[3 * C :, :] = dot(act0_ref[:rows, : 3 * C], delta1_ref[:rows, :C], 0, 0)
    gf_ref[3 * C :, :] += dot(act0_ref[:rows, 2 * C :], delta1_ref[:rows, C:], 0, 0)
    launch(1)
    launch(2)
    absorb(0)
    launch(0)
    t0_ref[...] = dot(delta1_ref[:, :C], w1_ref[...], 1, 1)
    t1_ref[...] = dot(delta1_ref[:, C:], w1_ref[...], 1, 1)
    for part in (1, 2):
        absorb(part)
        launch(part)
    t1_ref[:, 2 * C :] = pltpu.roll(t1_ref[:, 2 * C :], 1, 0)

    def back(i, carry):
        one, two = carry
        at = pl.ds(pl.multiple_of(i * STEP, STEP), STEP)
        grads = (
            t0_ref[at, :C] + t1_ref[at, 2 * C :],
            t0_ref[at, C : 2 * C],
            t0_ref[at, 2 * C :] + t1_ref[at, :C],
            t1_ref[at, C : 2 * C],
        )
        for q in range(4):
            lanes = slice(q * C, (q + 1) * C)
            dnorm = grads[q] * slope0_ref[at, lanes]
            dn_ref[at, lanes] = dnorm
            one = one + dnorm
            two = two + dnorm * norm_ref[at, lanes]
        return one, two

    one, two = lax.fori_loop(0, rows // STEP, back, (zero, zero))
    local_one = jnp.sum(one, 0, keepdims=True)
    local_two = jnp.sum(two, 0, keepdims=True)
    stat_ref[1, 0:1, :] = local_one
    stat_ref[1, 1:2, :] = local_two
    copies = share(1)
    absorb(0)
    launch(0)
    total = gathered(1, copies)
    mean_one, mean_two = total[0:1] / count, total[1:2] / count
    scale = gain * inverse

    def through_norm(i, carry):
        at = pl.ds(pl.multiple_of(i * STEP, STEP), STEP)
        for q in range(4):
            lanes = slice(q * C, (q + 1) * C)
            dn_ref[at, lanes] = scale * (dn_ref[at, lanes] - mean_one - norm_ref[at, lanes] * mean_two)
        return carry

    lax.fori_loop(0, rows // STEP, through_norm, 0)
    grad_zero = jnp.zeros((16, C), F32)
    for q in range(4):
        grad_zero = grad_zero + dot(patches_ref[q, :rows], dn_ref[:, q * C : (q + 1) * C], 0, 0, HIGH)
    little[0] = grad_zero
    little[0, 10:11, :] = local_two
    little[0, 11:12, :] = local_one

    small_copies = []

    def launch_small():
        step = len(small_copies)
        copy = pltpu.make_async_remote_copy(
            src_ref=little.at[step],
            dst_ref=little_in.at[step],
            send_sem=sm_send.at[step],
            recv_sem=sm_recv.at[step],
            device_id=partner(orders[0][step]),
            device_id_type=MESH,
        )
        copy.start()
        small_copies.append(copy)

    def absorb_small():
        step = len(small_copies) - 1
        small_copies[-1].wait_recv()
        little[step + 1] = little[step] + little_in[step]

    stages = len(orders[0])
    launch_small()
    while min(len(s[3]) for s in state) < stages:
        for part in range(3):
            if len(state[part][3]) < stages:
                absorb(part)
                launch(part)
        if len(small_copies) < stages:
            absorb_small()
            launch_small()

    for part in range(3):
        absorb(part)
        narrow(res_ref, gf_ref, state[part][1], state[part][0])

    gathers = [[] for _ in range(3)]
    for step in range(stages - 1, -1, -1):
        for part in range(3):
            if gathers[part]:
                gathers[part][-1].wait_recv()
            _, keep, size, start, half = state[part][3][step]
            if half == size:
                continue
            piece = pl.ds(pl.multiple_of(keep, 16), half)
            copy = pltpu.make_async_remote_copy(
                src_ref=res_ref.at[piece, :],
                dst_ref=res_ref.at[piece, :],
                send_sem=rs_send.at[part, stages + step],
                recv_sem=rs_recv.at[part, stages + step],
                device_id=partner(orders[part][step]),
                device_id_type=MESH,
            )
            copy.start()
            gathers[part].append(copy)
        if len(small_copies) < stages:
            absorb_small()
            launch_small()
    while len(small_copies) < stages:
        absorb_small()
        launch_small()
    absorb_small()
    small_ref[...] = little[stages]
    for part in range(3):
        gathers[part][-1].wait_recv()
        for copy in gathers[part]:
            copy.wait_send()
        for copy, _, size, _, half in state[part][3]:
            if half < size:
                copy.wait_send()
    for copy in small_copies:
        copy.wait_send()


def shards(tm, rec, audio, conv0_weight, norm_gain, norm_bias, conv1_weight, conv2_weight, cotangent):
    samples = audio.shape[1]
    rows = samples // 20
    rows_all = rows + EDGE
    C = conv0_weight.shape[1]
    after = from_behind(audio[:, :20], "tm", -1)
    ahead = from_behind(audio[:, -20:], "tm", 1)
    cot_edge = from_behind(cotangent[0, -1:, :], "tm", 1)
    lines = jnp.concatenate(
        [audio.reshape(rows, 20), after, jnp.zeros((EDGE - 2, 20), F32), ahead], 0
    )
    wide = jnp.concatenate([lines, jnp.concatenate([lines[1:, :5], lines[:1, :5]], 0), jnp.zeros((rows_all, 6), F32)], 1)
    patches = jnp.stack([wide[:, 5 * q : 5 * q + 16] for q in range(4)], 0)
    taps = jnp.concatenate([conv0_weight, jnp.zeros((6, C), F32)], 0)
    keep = (lax.broadcasted_iota(jnp.int32, (1, 1, 16), 2) < 10).astype(F32)
    patches = patches * keep
    cot = jnp.concatenate([cotangent[0], jnp.zeros((EDGE - 1, C), BF16), cot_edge], 0)
    stages = (tm.bit_length() - 1) + (rec.bit_length() - 1)
    total_rows = 6 * C
    vmem = pl.BlockSpec(memory_space=pltpu.VMEM)
    features, res, small = pl.pallas_call(
        functools.partial(kernel, tm, rec),
        out_shape=(
            jax.ShapeDtypeStruct((rows, C), BF16),
            jax.ShapeDtypeStruct((total_rows, C), BF16),
            jax.ShapeDtypeStruct((16, C), F32),
        ),
        in_specs=[vmem] * 7,
        out_specs=(vmem,) * 3,
        scratch_shapes=[
            pltpu.VMEM((rows_all, 4 * C), F32),
            pltpu.VMEM((rows_all, 4 * C), F32),
            pltpu.VMEM((rows_all, 5 * C), BF16),
            pltpu.VMEM((rows_all, 2 * C), F32),
            pltpu.VMEM((rows_all, 2 * C), F32),
            pltpu.VMEM((rows_all, 3 * C), BF16),
            pltpu.VMEM((rows_all, C), F32),
            pltpu.VMEM((rows_all, C), BF16),
            pltpu.VMEM((rows_all, 2 * C), BF16),
            pltpu.VMEM((rows, 4 * C), F32),
            pltpu.VMEM((rows_all, 3 * C), F32),
            pltpu.VMEM((rows_all, 3 * C), F32),
            pltpu.VMEM((total_rows, C), F32),
            pltpu.VMEM((total_rows, C), BF16),
            pltpu.VMEM((3, total_rows // 3 + 64, C), BF16),
            pltpu.VMEM((2, 2, C), F32),
            pltpu.VMEM((2, tm, 2, C), F32),
            pltpu.VMEM((stages + 1, 16, C), F32),
            pltpu.VMEM((stages, 16, C), F32),
            pltpu.SemaphoreType.DMA((3, 2 * stages)),
            pltpu.SemaphoreType.DMA((3, 2 * stages)),
            pltpu.SemaphoreType.DMA((2, tm)),
            pltpu.SemaphoreType.DMA((2, tm)),
            pltpu.SemaphoreType.DMA((stages,)),
            pltpu.SemaphoreType.DMA((stages,)),
        ],
        compiler_params=pltpu.CompilerParams(
            collective_id=0, has_side_effects=True, vmem_limit_bytes=52 * 2**20
        ),
    )(patches, taps, norm_gain[None, :], norm_bias[None, :], conv1_weight, conv2_weight, cot)
    grad_two = res[: 3 * C].astype(F32)
    grad_one = res[3 * C :].astype(F32)
    return (features[None], small[:10], small[10], small[11], grad_one, grad_two)


def solution(mesh):
    return jax.shard_map(
        functools.partial(shards, mesh.shape["tm"], mesh.shape["rec"]),
        mesh=mesh,
        in_specs=(P("rec", "tm"), P(), P(), P(), P(), P(), P("rec", "tm", None)),
        out_specs=(P("rec", "tm", None), P(), P(), P(), P(), P()),
        check_vma=False,
    )
```

```python
import functools

import jax
import jax.numpy as jnp
from jax import lax
from jax.experimental import pallas as pl
from jax.experimental.pallas import tpu as pltpu
from jax.sharding import PartitionSpec as P

EPS = 1e-05
HIGH = lax.Precision.HIGHEST
MESH = pl.DeviceIdType.MESH
F32, BF16 = jnp.float32, jnp.bfloat16
EDGE = 16
STEP = 16


def gelu_parts(value):
    phi = 0.5 * (1.0 + lax.erf(value * 0.7071067811865476))
    slope = phi + value * jnp.exp(-0.5 * value * value) * 0.3989422804014327
    return value * phi, slope


def dot(a, b, ca, cb, precision=None):
    return lax.dot_general(
        a, b, (((ca,), (cb,)), ((), ())), precision=precision, preferred_element_type=F32
    )


def plan(tm, rec):
    inner = [("tm", 1 << i) for i in range(1, tm.bit_length() - 1)]
    low, high = inner[: len(inner) // 2], inner[len(inner) // 2 :]
    outer = [("rec", 1 << i) for i in range(rec.bit_length() - 1)]
    core = [("tm", 1)]
    one, two = core + low + high + outer, core + high + low + outer
    return [one, two, core + outer + low + high, one, two, core + outer + high + low]


def kernel(
    tm, rec, audio_ref, taps_ref, gain_ref, bias_ref, w1_ref, w2_ref, cot_ref,
    features_ref, res_ref, small_ref,
    norm_ref, slope0_ref, act0_ref, pre1_ref, slope1_ref, act1_ref, pre2_ref, delta2_ref, delta1_ref,
    x_ref, xx_ref, wide_ref, edge_ref, dn_ref, t0_ref, t1_ref, gf_ref, sendbuf, recvbuf, stat_ref, stat_in, little, little_in,
    ed_send, ed_recv, rs_send, rs_recv, st_send, st_recv, sm_send, sm_recv,
):
    me = {"tm": lax.axis_index("tm"), "rec": lax.axis_index("rec")}
    rows_all, channels = norm_ref.shape[0], gain_ref.shape[1]
    rows = rows_all - EDGE
    count = 4.0 * rows * tm
    orders = plan(tm, rec)
    stages, parts = len(orders[0]), len(orders)
    share_rows = gf_ref.shape[0] // parts
    C = channels

    def bit_of(stage):
        axis, bit = stage
        return lax.rem(me[axis] // bit, 2)

    def partner(stage):
        axis, bit = stage
        return {axis: me[axis] + bit * (1 - 2 * bit_of(stage))}

    barrier = pltpu.get_barrier_semaphore()
    rec_bits = [s for s in orders[0] if s[0] == "rec"]
    for d in range(1, tm):
        pl.semaphore_signal(barrier, inc=1, device_id={"tm": lax.rem(me["tm"] + d, tm)}, device_id_type=MESH)
    for stage in rec_bits:
        pl.semaphore_signal(barrier, inc=1, device_id=partner(stage), device_id_type=MESH)

    x_ref[:rows, :] = audio_ref[...]
    for q in range(4):
        wide = taps_ref[...] if q == 0 else pltpu.roll(taps_ref[...], 5 * q, 0)
        wide_ref[:, q * C : (q + 1) * C] = wide
    pl.semaphore_wait(barrier, tm - 1 + len(rec_bits))
    behind, ahead = lax.rem(me["tm"] + 1, tm), lax.rem(me["tm"] + tm - 1, tm)
    edges = []
    for i, (source, target, device) in enumerate((
        (x_ref.at[0:8, :], x_ref.at[rows : rows + 8, :], ahead),
        (x_ref.at[rows - 8 : rows, :], x_ref.at[rows + 8 : rows + 16, :], behind),
        (cot_ref.at[rows - 16 : rows, :], edge_ref, behind),
    )):
        copy = pltpu.make_async_remote_copy(
            src_ref=source, dst_ref=target, send_sem=ed_send.at[i], recv_sem=ed_recv.at[i],
            device_id={"tm": device}, device_id_type=MESH,
        )
        copy.start()
        edges.append(copy)
    for copy in edges:
        copy.wait()

    row = lax.broadcasted_iota(jnp.int32, x_ref.shape, 0)
    lane = lax.broadcasted_iota(jnp.int32, x_ref.shape, 1)
    outside = jnp.logical_or(
        jnp.logical_and(row >= rows + 8, me["tm"] == 0),
        jnp.logical_and(jnp.logical_and(row >= rows, row < rows + 8), me["tm"] == tm - 1),
    )
    x = jnp.where(outside, 0.0, x_ref[...])
    next_row = jnp.where(lane < 5, pltpu.roll(x, rows_all - 1, 0), 0.0)
    xx_ref[...] = x + pltpu.roll(next_row, 20, 1)
    for q in range(4):
        lanes = slice(q * C, (q + 1) * C)
        norm_ref[:, lanes] = dot(xx_ref[:, :32], wide_ref[:, lanes], 1, 0, HIGH)

    def sums(i, carry):
        one, two = carry
        for q in range(4):
            part = norm_ref[pl.ds(i * STEP, STEP), q * C : (q + 1) * C]
            one, two = one + part, two + part * part
        return one, two

    zero = jnp.zeros((STEP, C), F32)
    one, two = lax.fori_loop(0, rows // STEP, sums, (zero, zero))
    stat_ref[0, 0:1, :] = jnp.sum(one, 0, keepdims=True)
    stat_ref[0, 1:2, :] = jnp.sum(two, 0, keepdims=True)

    def share(which):
        copies = []
        for d in range(1, tm):
            copy = pltpu.make_async_remote_copy(
                src_ref=stat_ref.at[which],
                dst_ref=stat_in.at[which, d],
                send_sem=st_send.at[which, d],
                recv_sem=st_recv.at[which, d],
                device_id={"tm": lax.rem(me["tm"] + d, tm)},
                device_id_type=MESH,
            )
            copy.start()
            copies.append(copy)
        return copies

    def gathered(which, copies):
        total = stat_ref[which]
        for d, copy in enumerate(copies):
            copy.wait_recv()
            total = total + stat_in[which, d + 1]
        for copy in copies:
            copy.wait_send()
        return total

    total = gathered(0, share(0))
    mean = total[0:1] / count
    variance = total[1:2] / count - mean * mean
    inverse = lax.rsqrt(variance + EPS)
    gain, bias = gain_ref[...], bias_ref[...]

    def first_act(i, carry):
        at = pl.ds(pl.multiple_of(i * STEP, STEP), STEP)
        row = i * STEP + lax.broadcasted_iota(jnp.int32, (STEP, C), 0)
        past = jnp.logical_and(row == rows, me["tm"] == tm - 1)
        for q in range(4):
            lanes = slice(q * C, (q + 1) * C)
            normed = (norm_ref[at, lanes] - mean) * inverse
            norm_ref[at, lanes] = normed
            act, slope = gelu_parts(normed * gain + bias)
            act0_ref[at, lanes] = jnp.where(past, 0.0, act).astype(BF16)
            slope0_ref[at, lanes] = slope
        return carry

    lax.fori_loop(0, rows_all // STEP, first_act, 0)
    act0_ref[:, 4 * C :] = pltpu.roll(act0_ref[:, :C].astype(F32), rows_all - 1, 0).astype(BF16)

    pre1_ref[:, :C] = dot(act0_ref[:, : 3 * C], w1_ref[...], 1, 0)
    pre1_ref[:, C:] = dot(act0_ref[:, 2 * C :], w1_ref[...], 1, 0)

    def second_act(i, carry):
        at = pl.ds(pl.multiple_of(i * STEP, STEP), STEP)
        row = i * STEP + lax.broadcasted_iota(jnp.int32, (STEP, 2 * C), 0)
        past = jnp.logical_and(row == rows, me["tm"] == tm - 1)
        act, slope = gelu_parts(pre1_ref[at, :])
        act1_ref[at, : 2 * C] = jnp.where(past, 0.0, act).astype(BF16)
        slope1_ref[at, :] = slope
        return carry

    lax.fori_loop(0, rows_all // STEP, second_act, 0)
    act1_ref[:, 2 * C :] = pltpu.roll(act1_ref[:, :C].astype(F32), rows_all - 1, 0).astype(BF16)

    pre2_ref[...] = dot(act1_ref[...], w2_ref[...], 1, 0)

    def third_act(i, carry):
        at = pl.ds(pl.multiple_of(i * STEP, STEP), STEP)
        act, slope = gelu_parts(pre2_ref[at, :])
        features_ref[at, :] = act.astype(BF16)
        delta2_ref[at, :] = (cot_ref[at, :].astype(F32) * slope).astype(BF16)
        return carry

    lax.fori_loop(0, rows // STEP, third_act, 0)
    slope = gelu_parts(pre2_ref[rows:, :])[1]
    edge = jnp.where(me["tm"] == 0, 0.0, edge_ref[...].astype(F32))
    delta2_ref[rows:, :] = (edge * slope).astype(BF16)

    state = [{"size": share_rows, "start": p * share_rows, "used": 0, "step": 0, "sent": [], "back": []} for p in range(parts)]

    def combine(target, part, start, size, came_at):
        block = min(32, size)

        def body(i, carry):
            at = pl.ds(pl.multiple_of(start + i * block, 16), block)
            value = gf_ref[at, :]
            if came_at is not None:
                value = value + recvbuf[part, pl.ds(pl.multiple_of(came_at + i * block, 16), block), :].astype(F32)
            target[at, :] = value.astype(target.dtype)
            return carry

        lax.fori_loop(0, size // block, body, 0)

    def send_piece(part, ref_from, ref_to, index, stage):
        copy = pltpu.make_async_remote_copy(
            src_ref=ref_from, dst_ref=ref_to,
            send_sem=rs_send.at[part, index], recv_sem=rs_recv.at[part, index],
            device_id=partner(stage), device_id_type=MESH,
        )
        copy.start()
        return copy

    def advance(part):
        s = state[part]
        step, size, start = s["step"], s["size"], s["start"]
        s["step"] += 1
        if step <= stages:
            base = None
            if step > 0:
                last, _, _, last_half, whole = s["sent"][-1]
                last.wait_recv()
                if whole:
                    last.wait_send()
                base = s["used"] - last_half
        if step < stages:
            stage = orders[part][step]
            whole = size // 2 < 16
            if whole:
                half, keep, away = size, start, start
                if base is not None:
                    combine(gf_ref, part, start, size, base)
                combine(sendbuf, part, start, size, None)
            else:
                half, bit = size // 2, bit_of(stage)
                keep, away = start + bit * half, start + (1 - bit) * half
                combine(sendbuf, part, away, half, None if base is None else base + (1 - bit) * half)
            copy = send_piece(
                part,
                sendbuf.at[pl.ds(pl.multiple_of(away, 16), half), :],
                recvbuf.at[part, pl.ds(s["used"], half), :],
                step, stage,
            )
            if not whole and base is not None:
                combine(gf_ref, part, keep, half, base + bit * half)
            s["sent"].append((copy, keep, size, half, whole))
            s["size"], s["start"], s["used"] = half, keep, s["used"] + half
            return
        if step == stages:
            combine(res_ref, part, start, size, base)
        elif s["back"]:
            s["back"][-1].wait_recv()
        index = 2 * stages - 1 - step
        if index >= 0:
            _, keep, _, half, whole = s["sent"][index]
            if not whole:
                piece = res_ref.at[pl.ds(pl.multiple_of(keep, 16), half), :]
                s["back"].append(send_piece(part, piece, piece, stages + index, orders[part][index]))

    gf_ref[: 3 * C, :] = dot(act1_ref[:rows, :], delta2_ref[:rows, :], 0, 0)
    for part in (0, 1, 2):
        advance(part)
    t0_ref[...] = dot(delta2_ref[...], w2_ref[...], 1, 1)
    even = t0_ref[:, :C] + pltpu.roll(t0_ref[:, 2 * C :], 1, 0)
    delta1_ref[:, :C] = (even * slope1_ref[:, :C]).astype(BF16)
    delta1_ref[:, C:] = (t0_ref[:, C : 2 * C] * slope1_ref[:, C:]).astype(BF16)
    for part in (0, 1, 2):
        advance(part)

    gf_ref[3 * C :, :] = dot(act0_ref[:rows, : 3 * C], delta1_ref[:rows, :C], 0, 0)
    gf_ref[3 * C :, :] += dot(act0_ref[:rows, 2 * C :], delta1_ref[:rows, C:], 0, 0)
    for part in (3, 4, 5):
        advance(part)
    t0_ref[...] = dot(delta1_ref[:, :C], w1_ref[...], 1, 1)
    t1_ref[...] = dot(delta1_ref[:, C:], w1_ref[...], 1, 1)
    for part in (0, 3, 1, 4, 2, 5):
        advance(part)
    t1_ref[:, 2 * C :] = pltpu.roll(t1_ref[:, 2 * C :], 1, 0)

    def back(i, carry):
        one, two = carry
        at = pl.ds(pl.multiple_of(i * STEP, STEP), STEP)
        grads = (
            t0_ref[at, :C] + t1_ref[at, 2 * C :],
            t0_ref[at, C : 2 * C],
            t0_ref[at, 2 * C :] + t1_ref[at, :C],
            t1_ref[at, C : 2 * C],
        )
        for q in range(4):
            lanes = slice(q * C, (q + 1) * C)
            dnorm = grads[q] * slope0_ref[at, lanes]
            dn_ref[at, lanes] = dnorm
            one = one + dnorm
            two = two + dnorm * norm_ref[at, lanes]
        return one, two

    one, two = lax.fori_loop(0, rows // STEP, back, (zero, zero))
    local_one = jnp.sum(one, 0, keepdims=True)
    local_two = jnp.sum(two, 0, keepdims=True)
    stat_ref[1, 0:1, :] = local_one
    stat_ref[1, 1:2, :] = local_two
    copies = share(1)
    for part in (0, 1, 2):
        advance(part)
    total = gathered(1, copies)
    mean_one, mean_two = total[0:1] / count, total[1:2] / count
    scale = gain * inverse

    def through_norm(i, carry):
        at = pl.ds(pl.multiple_of(i * STEP, STEP), STEP)
        for q in range(4):
            lanes = slice(q * C, (q + 1) * C)
            dn_ref[at, lanes] = scale * (dn_ref[at, lanes] - mean_one - norm_ref[at, lanes] * mean_two)
        return carry

    lax.fori_loop(0, rows // STEP, through_norm, 0)
    for part in (3, 4, 5):
        advance(part)
    grad_zero = jnp.zeros((32, C), F32)
    for q in range(4):
        taps = dot(xx_ref[:rows, :32], dn_ref[:, q * C : (q + 1) * C], 0, 0, HIGH)
        grad_zero = grad_zero + (taps if q == 0 else pltpu.roll(taps, 32 - 5 * q, 0))
    little[0] = grad_zero[:16]
    little[0, 10:11, :] = local_two
    little[0, 11:12, :] = local_one

    small_copies = []

    def launch_small():
        step = len(small_copies)
        copy = pltpu.make_async_remote_copy(
            src_ref=little.at[step],
            dst_ref=little_in.at[step],
            send_sem=sm_send.at[step],
            recv_sem=sm_recv.at[step],
            device_id=partner(orders[0][step]),
            device_id_type=MESH,
        )
        copy.start()
        small_copies.append(copy)

    def absorb_small():
        step = len(small_copies) - 1
        small_copies[-1].wait_recv()
        little[step + 1] = little[step] + little_in[step]

    launch_small()
    while min(s["step"] for s in state) <= 2 * stages:
        for part in range(parts):
            if state[part]["step"] <= 2 * stages:
                advance(part)
        if len(small_copies) < stages:
            absorb_small()
            launch_small()
    while len(small_copies) < stages:
        absorb_small()
        launch_small()
    absorb_small()
    small_ref[...] = little[stages]
    for s in state:
        for copy in s["back"]:
            copy.wait_send()
        for copy, _, _, _, whole in s["sent"]:
            if not whole:
                copy.wait_send()
    for copy in small_copies:
        copy.wait_send()


def shards(tm, rec, audio, conv0_weight, norm_gain, norm_bias, conv1_weight, conv2_weight, cotangent):
    samples = audio.shape[1]
    rows = samples // 20
    rows_all = rows + EDGE
    C = conv0_weight.shape[1]
    lines = jnp.pad(audio.reshape(rows, 20), ((0, 0), (0, 108)))
    taps = jnp.concatenate([conv0_weight, jnp.zeros((22, C), F32)], 0)
    stages = (tm.bit_length() - 1) + (rec.bit_length() - 1)
    total_rows = 6 * C
    vmem = pl.BlockSpec(memory_space=pltpu.VMEM)
    features, res, small = pl.pallas_call(
        functools.partial(kernel, tm, rec),
        out_shape=(
            jax.ShapeDtypeStruct((rows, C), BF16),
            jax.ShapeDtypeStruct((total_rows, C), BF16),
            jax.ShapeDtypeStruct((16, C), F32),
        ),
        in_specs=[vmem] * 7,
        out_specs=(vmem,) * 3,
        scratch_shapes=[
            pltpu.VMEM((rows_all, 4 * C), F32),
            pltpu.VMEM((rows_all, 4 * C), F32),
            pltpu.VMEM((rows_all, 5 * C), BF16),
            pltpu.VMEM((rows_all, 2 * C), F32),
            pltpu.VMEM((rows_all, 2 * C), F32),
            pltpu.VMEM((rows_all, 3 * C), BF16),
            pltpu.VMEM((rows_all, C), F32),
            pltpu.VMEM((rows_all, C), BF16),
            pltpu.VMEM((rows_all, 2 * C), BF16),
            pltpu.VMEM((rows_all, 128), F32),
            pltpu.VMEM((rows_all, 128), F32),
            pltpu.VMEM((32, 4 * C), F32),
            pltpu.VMEM((EDGE, C), BF16),
            pltpu.VMEM((rows, 4 * C), F32),
            pltpu.VMEM((rows_all, 3 * C), F32),
            pltpu.VMEM((rows_all, 3 * C), F32),
            pltpu.VMEM((total_rows, C), F32),
            pltpu.VMEM((total_rows, C), BF16),
            pltpu.VMEM((6, total_rows // 6 + 96, C), BF16),
            pltpu.VMEM((2, 2, C), F32),
            pltpu.VMEM((2, tm, 2, C), F32),
            pltpu.VMEM((stages + 1, 16, C), F32),
            pltpu.VMEM((stages, 16, C), F32),
            pltpu.SemaphoreType.DMA((3,)),
            pltpu.SemaphoreType.DMA((3,)),
            pltpu.SemaphoreType.DMA((6, 2 * stages)),
            pltpu.SemaphoreType.DMA((6, 2 * stages)),
            pltpu.SemaphoreType.DMA((2, tm)),
            pltpu.SemaphoreType.DMA((2, tm)),
            pltpu.SemaphoreType.DMA((stages,)),
            pltpu.SemaphoreType.DMA((stages,)),
        ],
        compiler_params=pltpu.CompilerParams(
            collective_id=0, has_side_effects=True, vmem_limit_bytes=52 * 2**20
        ),
    )(lines, taps, norm_gain[None, :], norm_bias[None, :], conv1_weight, conv2_weight, cotangent[0])
    grad_two = res[: 3 * C].astype(F32)
    grad_one = res[3 * C :].astype(F32)
    return (features[None], small[:10], small[10], small[11], grad_one, grad_two)


def solution(mesh):
    return jax.shard_map(
        functools.partial(shards, mesh.shape["tm"], mesh.shape["rec"]),
        mesh=mesh,
        in_specs=(P("rec", "tm"), P(), P(), P(), P(), P(), P("rec", "tm", None)),
        out_specs=(P("rec", "tm", None), P(), P(), P(), P(), P()),
        check_vma=False,
    )
```

```python
import functools

import jax
import jax.numpy as jnp
from jax import lax
from jax.experimental import pallas as pl
from jax.experimental.pallas import tpu as pltpu
from jax.sharding import PartitionSpec as P

EPS = 1e-05
HIGH = lax.Precision.HIGHEST
MESH = pl.DeviceIdType.MESH
F32, BF16 = jnp.float32, jnp.bfloat16
EDGE = 16
STEP = 16


def gelu_parts(value):
    phi = 0.5 * (1.0 + lax.erf(value * 0.7071067811865476))
    slope = phi + value * jnp.exp(-0.5 * value * value) * 0.3989422804014327
    return value * phi, slope


def dot(a, b, ca, cb, precision=None):
    return lax.dot_general(
        a, b, (((ca,), (cb,)), ((), ())), precision=precision, preferred_element_type=F32
    )


def plan(tm, rec):
    inner = [("tm", 1 << i) for i in range(1, tm.bit_length() - 1)]
    low, high = inner[: len(inner) // 2], inner[len(inner) // 2 :]
    outer = [("rec", 1 << i) for i in range(rec.bit_length() - 1)]
    core = [("tm", 1)]
    one, two = core + low + high + outer, core + high + low + outer
    return [one, two, core + outer + low + high, one, two, core + outer + high + low]


def kernel(
    tm, rec, audio_ref, taps_ref, gain_ref, bias_ref, w1_hbm, w2_hbm, cot_ref,
    features_ref, res_ref, small_ref,
    norm_ref, slope0_ref, act0_ref, pre1_ref, slope1_ref, act1_ref, pre2_ref, delta2_ref, delta1_ref,
    x_ref, xx_ref, wide_ref, edge_ref, dn_ref, t0_ref, t1_ref, gf_ref, sendbuf, recvbuf, stat_ref, stat_in, little, little_in,
    w1_ref, w2_ref, load_sem, ed_send, ed_recv, rs_send, rs_recv, st_send, st_recv, sm_send, sm_recv,
):
    me = {"tm": lax.axis_index("tm"), "rec": lax.axis_index("rec")}
    rows_all, channels = norm_ref.shape[0], gain_ref.shape[1]
    rows = rows_all - EDGE
    count = 4.0 * rows * tm
    orders = plan(tm, rec)
    stages, parts = len(orders[0]), len(orders)
    share_rows = gf_ref.shape[0] // parts
    C = channels

    def bit_of(stage):
        axis, bit = stage
        return lax.rem(me[axis] // bit, 2)

    def partner(stage):
        axis, bit = stage
        return {axis: me[axis] + bit * (1 - 2 * bit_of(stage))}

    loads = [
        pltpu.make_async_copy(w1_hbm, w1_ref, load_sem.at[0]),
        pltpu.make_async_copy(w2_hbm, w2_ref, load_sem.at[1]),
    ]
    for load in loads:
        load.start()
    barrier = pltpu.get_barrier_semaphore()
    rec_bits = [s for s in orders[0] if s[0] == "rec"]
    for d in range(1, tm):
        pl.semaphore_signal(barrier, inc=1, device_id={"tm": lax.rem(me["tm"] + d, tm)}, device_id_type=MESH)
    for stage in rec_bits:
        pl.semaphore_signal(barrier, inc=1, device_id=partner(stage), device_id_type=MESH)

    x_ref[:rows, :] = audio_ref[...]
    for q in range(4):
        wide = taps_ref[...] if q == 0 else pltpu.roll(taps_ref[...], 5 * q, 0)
        wide_ref[:, q * C : (q + 1) * C] = wide
    pl.semaphore_wait(barrier, tm - 1 + len(rec_bits))
    behind, ahead = lax.rem(me["tm"] + 1, tm), lax.rem(me["tm"] + tm - 1, tm)
    edges = []
    for i, (source, target, device) in enumerate((
        (x_ref.at[0:8, :], x_ref.at[rows : rows + 8, :], ahead),
        (x_ref.at[rows - 8 : rows, :], x_ref.at[rows + 8 : rows + 16, :], behind),
        (cot_ref.at[rows - 16 : rows, :], edge_ref, behind),
    )):
        copy = pltpu.make_async_remote_copy(
            src_ref=source, dst_ref=target, send_sem=ed_send.at[i], recv_sem=ed_recv.at[i],
            device_id={"tm": device}, device_id_type=MESH,
        )
        copy.start()
        edges.append(copy)
    for copy in edges[:2]:
        copy.wait()

    row = lax.broadcasted_iota(jnp.int32, x_ref.shape, 0)
    lane = lax.broadcasted_iota(jnp.int32, x_ref.shape, 1)
    outside = jnp.logical_or(
        jnp.logical_and(row >= rows + 8, me["tm"] == 0),
        jnp.logical_and(jnp.logical_and(row >= rows, row < rows + 8), me["tm"] == tm - 1),
    )
    x = jnp.where(outside, 0.0, x_ref[...])
    next_row = jnp.where(lane < 5, pltpu.roll(x, rows_all - 1, 0), 0.0)
    xx_ref[...] = x + pltpu.roll(next_row, 20, 1)
    for q in range(4):
        lanes = slice(q * C, (q + 1) * C)
        norm_ref[:, lanes] = dot(xx_ref[:, :32], wide_ref[:, lanes], 1, 0, HIGH)

    def sums(i, carry):
        one, two = carry
        for q in range(4):
            part = norm_ref[pl.ds(i * STEP, STEP), q * C : (q + 1) * C]
            one, two = one + part, two + part * part
        return one, two

    zero = jnp.zeros((STEP, C), F32)
    one, two = lax.fori_loop(0, rows // STEP, sums, (zero, zero))
    stat_ref[0, 0:1, :] = jnp.sum(one, 0, keepdims=True)
    stat_ref[0, 1:2, :] = jnp.sum(two, 0, keepdims=True)

    def share(which):
        copies = []
        for d in range(1, tm):
            copy = pltpu.make_async_remote_copy(
                src_ref=stat_ref.at[which],
                dst_ref=stat_in.at[which, d],
                send_sem=st_send.at[which, d],
                recv_sem=st_recv.at[which, d],
                device_id={"tm": lax.rem(me["tm"] + d, tm)},
                device_id_type=MESH,
            )
            copy.start()
            copies.append(copy)
        return copies

    def gathered(which, copies):
        total = stat_ref[which]
        for d, copy in enumerate(copies):
            copy.wait_recv()
            total = total + stat_in[which, d + 1]
        for copy in copies:
            copy.wait_send()
        return total

    total = gathered(0, share(0))
    mean = total[0:1] / count
    variance = total[1:2] / count - mean * mean
    inverse = lax.rsqrt(variance + EPS)
    gain, bias = gain_ref[...], bias_ref[...]

    def first_act(i, carry):
        at = pl.ds(pl.multiple_of(i * STEP, STEP), STEP)
        row = i * STEP + lax.broadcasted_iota(jnp.int32, (STEP, C), 0)
        past = jnp.logical_and(row == rows, me["tm"] == tm - 1)
        for q in range(4):
            lanes = slice(q * C, (q + 1) * C)
            normed = (norm_ref[at, lanes] - mean) * inverse
            norm_ref[at, lanes] = normed
            act, slope = gelu_parts(normed * gain + bias)
            act0_ref[at, lanes] = jnp.where(past, 0.0, act).astype(BF16)
            slope0_ref[at, lanes] = slope
        return carry

    lax.fori_loop(0, rows_all // STEP, first_act, 0)
    act0_ref[:, 4 * C :] = pltpu.roll(act0_ref[:, :C].astype(F32), rows_all - 1, 0).astype(BF16)

    loads[0].wait()
    pre1_ref[:, :C] = dot(act0_ref[:, : 3 * C], w1_ref[...], 1, 0)
    pre1_ref[:, C:] = dot(act0_ref[:, 2 * C :], w1_ref[...], 1, 0)

    def second_act(i, carry):
        at = pl.ds(pl.multiple_of(i * STEP, STEP), STEP)
        row = i * STEP + lax.broadcasted_iota(jnp.int32, (STEP, 2 * C), 0)
        past = jnp.logical_and(row == rows, me["tm"] == tm - 1)
        act, slope = gelu_parts(pre1_ref[at, :])
        act1_ref[at, : 2 * C] = jnp.where(past, 0.0, act).astype(BF16)
        slope1_ref[at, :] = slope
        return carry

    lax.fori_loop(0, rows_all // STEP, second_act, 0)
    act1_ref[:, 2 * C :] = pltpu.roll(act1_ref[:, :C].astype(F32), rows_all - 1, 0).astype(BF16)

    loads[1].wait()
    pre2_ref[...] = dot(act1_ref[...], w2_ref[...], 1, 0)

    def third_act(i, carry):
        at = pl.ds(pl.multiple_of(i * STEP, STEP), STEP)
        act, slope = gelu_parts(pre2_ref[at, :])
        features_ref[at, :] = act.astype(BF16)
        delta2_ref[at, :] = (cot_ref[at, :].astype(F32) * slope).astype(BF16)
        return carry

    lax.fori_loop(0, rows // STEP, third_act, 0)
    edges[2].wait()
    slope = gelu_parts(pre2_ref[rows:, :])[1]
    edge = jnp.where(me["tm"] == 0, 0.0, edge_ref[...].astype(F32))
    delta2_ref[rows:, :] = (edge * slope).astype(BF16)

    state = [{"size": share_rows, "start": p * share_rows, "used": 0, "step": 0, "sent": [], "back": []} for p in range(parts)]

    def combine(target, part, start, size, came_at):
        block = min(32, size)

        def body(i, carry):
            at = pl.ds(pl.multiple_of(start + i * block, 16), block)
            value = gf_ref[at, :]
            if came_at is not None:
                value = value + recvbuf[part, pl.ds(pl.multiple_of(came_at + i * block, 16), block), :].astype(F32)
            target[at, :] = value.astype(target.dtype)
            return carry

        lax.fori_loop(0, size // block, body, 0)

    def send_piece(part, ref_from, ref_to, index, stage):
        copy = pltpu.make_async_remote_copy(
            src_ref=ref_from, dst_ref=ref_to,
            send_sem=rs_send.at[part, index], recv_sem=rs_recv.at[part, index],
            device_id=partner(stage), device_id_type=MESH,
        )
        copy.start()
        return copy

    def advance(part):
        s = state[part]
        step, size, start = s["step"], s["size"], s["start"]
        s["step"] += 1
        if step <= stages:
            base = None
            if step > 0:
                last, _, _, last_half, whole = s["sent"][-1]
                last.wait_recv()
                if whole:
                    last.wait_send()
                base = s["used"] - last_half
        if step < stages:
            stage = orders[part][step]
            whole = size // 2 < 16
            if whole:
                half, keep, away = size, start, start
                if base is not None:
                    combine(gf_ref, part, start, size, base)
                combine(sendbuf, part, start, size, None)
            else:
                half, bit = size // 2, bit_of(stage)
                keep, away = start + bit * half, start + (1 - bit) * half
                combine(sendbuf, part, away, half, None if base is None else base + (1 - bit) * half)
            copy = send_piece(
                part,
                sendbuf.at[pl.ds(pl.multiple_of(away, 16), half), :],
                recvbuf.at[part, pl.ds(s["used"], half), :],
                step, stage,
            )
            if not whole and base is not None:
                combine(gf_ref, part, keep, half, base + bit * half)
            s["sent"].append((copy, keep, size, half, whole))
            s["size"], s["start"], s["used"] = half, keep, s["used"] + half
            return
        if step == stages:
            combine(res_ref, part, start, size, base)
        elif s["back"]:
            s["back"][-1].wait_recv()
        index = 2 * stages - 1 - step
        if index >= 0:
            _, keep, _, half, whole = s["sent"][index]
            if not whole:
                piece = res_ref.at[pl.ds(pl.multiple_of(keep, 16), half), :]
                s["back"].append(send_piece(part, piece, piece, stages + index, orders[part][index]))

    gf_ref[: 3 * C, :] = dot(act1_ref[:rows, :], delta2_ref[:rows, :], 0, 0)
    for part in (0, 1, 2):
        advance(part)
    t0_ref[...] = dot(delta2_ref[...], w2_ref[...], 1, 1)
    even = t0_ref[:, :C] + pltpu.roll(t0_ref[:, 2 * C :], 1, 0)
    delta1_ref[:, :C] = (even * slope1_ref[:, :C]).astype(BF16)
    delta1_ref[:, C:] = (t0_ref[:, C : 2 * C] * slope1_ref[:, C:]).astype(BF16)
    for part in (0, 1, 2):
        advance(part)

    gf_ref[3 * C :, :] = dot(act0_ref[:rows, : 3 * C], delta1_ref[:rows, :C], 0, 0)
    gf_ref[3 * C :, :] += dot(act0_ref[:rows, 2 * C :], delta1_ref[:rows, C:], 0, 0)
    for part in (3, 4, 5):
        advance(part)
    t0_ref[...] = dot(delta1_ref[:, :C], w1_ref[...], 1, 1)
    t1_ref[...] = dot(delta1_ref[:, C:], w1_ref[...], 1, 1)
    for part in (0, 3, 1, 4, 2, 5):
        advance(part)
    t1_ref[:, 2 * C :] = pltpu.roll(t1_ref[:, 2 * C :], 1, 0)

    def back(i, carry):
        one, two = carry
        at = pl.ds(pl.multiple_of(i * STEP, STEP), STEP)
        grads = (
            t0_ref[at, :C] + t1_ref[at, 2 * C :],
            t0_ref[at, C : 2 * C],
            t0_ref[at, 2 * C :] + t1_ref[at, :C],
            t1_ref[at, C : 2 * C],
        )
        for q in range(4):
            lanes = slice(q * C, (q + 1) * C)
            dnorm = grads[q] * slope0_ref[at, lanes]
            dn_ref[at, lanes] = dnorm
            one = one + dnorm
            two = two + dnorm * norm_ref[at, lanes]
        return one, two

    one, two = lax.fori_loop(0, rows // STEP, back, (zero, zero))
    local_one = jnp.sum(one, 0, keepdims=True)
    local_two = jnp.sum(two, 0, keepdims=True)
    stat_ref[1, 0:1, :] = local_one
    stat_ref[1, 1:2, :] = local_two
    copies = share(1)
    for part in (0, 1, 2):
        advance(part)
    total = gathered(1, copies)
    mean_one, mean_two = total[0:1] / count, total[1:2] / count
    scale = gain * inverse

    def through_norm(i, carry):
        at = pl.ds(pl.multiple_of(i * STEP, STEP), STEP)
        for q in range(4):
            lanes = slice(q * C, (q + 1) * C)
            dn_ref[at, lanes] = scale * (dn_ref[at, lanes] - mean_one - norm_ref[at, lanes] * mean_two)
        return carry

    lax.fori_loop(0, rows // STEP, through_norm, 0)
    for part in (3, 4, 5):
        advance(part)
    grad_zero = jnp.zeros((32, C), F32)
    for q in range(4):
        taps = dot(xx_ref[:rows, :32], dn_ref[:, q * C : (q + 1) * C], 0, 0, HIGH)
        grad_zero = grad_zero + (taps if q == 0 else pltpu.roll(taps, 32 - 5 * q, 0))
    little[0] = grad_zero[:16]
    little[0, 10:11, :] = local_two
    little[0, 11:12, :] = local_one

    small_copies = []

    def launch_small():
        step = len(small_copies)
        copy = pltpu.make_async_remote_copy(
            src_ref=little.at[step],
            dst_ref=little_in.at[step],
            send_sem=sm_send.at[step],
            recv_sem=sm_recv.at[step],
            device_id=partner(orders[0][step]),
            device_id_type=MESH,
        )
        copy.start()
        small_copies.append(copy)

    def absorb_small():
        step = len(small_copies) - 1
        small_copies[-1].wait_recv()
        little[step + 1] = little[step] + little_in[step]

    launch_small()
    while min(s["step"] for s in state) <= 2 * stages:
        for part in (3, 4, 5, 0, 1, 2):
            if state[part]["step"] <= 2 * stages:
                advance(part)
        if len(small_copies) < stages:
            absorb_small()
            launch_small()
    while len(small_copies) < stages:
        absorb_small()
        launch_small()
    absorb_small()
    small_ref[...] = little[stages]
    for s in state:
        for copy in s["back"]:
            copy.wait_send()
        for copy, _, _, _, whole in s["sent"]:
            if not whole:
                copy.wait_send()
    for copy in small_copies:
        copy.wait_send()


def shards(tm, rec, audio, conv0_weight, norm_gain, norm_bias, conv1_weight, conv2_weight, cotangent):
    samples = audio.shape[1]
    rows = samples // 20
    rows_all = rows + EDGE
    C = conv0_weight.shape[1]
    lines = jnp.pad(audio.reshape(rows, 20), ((0, 0), (0, 108)))
    taps = jnp.concatenate([conv0_weight, jnp.zeros((22, C), F32)], 0)
    stages = (tm.bit_length() - 1) + (rec.bit_length() - 1)
    total_rows = 6 * C
    vmem = pl.BlockSpec(memory_space=pltpu.VMEM)
    features, res, small = pl.pallas_call(
        functools.partial(kernel, tm, rec),
        out_shape=(
            jax.ShapeDtypeStruct((rows, C), BF16),
            jax.ShapeDtypeStruct((total_rows, C), BF16),
            jax.ShapeDtypeStruct((16, C), F32),
        ),
        in_specs=[vmem] * 4 + [pl.BlockSpec(memory_space=pltpu.HBM)] * 2 + [vmem],
        out_specs=(vmem,) * 3,
        scratch_shapes=[
            pltpu.VMEM((rows_all, 4 * C), F32),
            pltpu.VMEM((rows_all, 4 * C), F32),
            pltpu.VMEM((rows_all, 5 * C), BF16),
            pltpu.VMEM((rows_all, 2 * C), F32),
            pltpu.VMEM((rows_all, 2 * C), F32),
            pltpu.VMEM((rows_all, 3 * C), BF16),
            pltpu.VMEM((rows_all, C), F32),
            pltpu.VMEM((rows_all, C), BF16),
            pltpu.VMEM((rows_all, 2 * C), BF16),
            pltpu.VMEM((rows_all, 128), F32),
            pltpu.VMEM((rows_all, 128), F32),
            pltpu.VMEM((32, 4 * C), F32),
            pltpu.VMEM((EDGE, C), BF16),
            pltpu.VMEM((rows, 4 * C), F32),
            pltpu.VMEM((rows_all, 3 * C), F32),
            pltpu.VMEM((rows_all, 3 * C), F32),
            pltpu.VMEM((total_rows, C), F32),
            pltpu.VMEM((total_rows, C), BF16),
            pltpu.VMEM((6, total_rows // 6 + 96, C), BF16),
            pltpu.VMEM((2, 2, C), F32),
            pltpu.VMEM((2, tm, 2, C), F32),
            pltpu.VMEM((stages + 1, 16, C), F32),
            pltpu.VMEM((stages, 16, C), F32),
            pltpu.VMEM((3 * C, C), BF16),
            pltpu.VMEM((3 * C, C), BF16),
            pltpu.SemaphoreType.DMA((2,)),
            pltpu.SemaphoreType.DMA((3,)),
            pltpu.SemaphoreType.DMA((3,)),
            pltpu.SemaphoreType.DMA((6, 2 * stages)),
            pltpu.SemaphoreType.DMA((6, 2 * stages)),
            pltpu.SemaphoreType.DMA((2, tm)),
            pltpu.SemaphoreType.DMA((2, tm)),
            pltpu.SemaphoreType.DMA((stages,)),
            pltpu.SemaphoreType.DMA((stages,)),
        ],
        compiler_params=pltpu.CompilerParams(
            collective_id=0, has_side_effects=True, vmem_limit_bytes=52 * 2**20
        ),
    )(lines, taps, norm_gain[None, :], norm_bias[None, :], conv1_weight, conv2_weight, cotangent[0])
    grad_two = res[: 3 * C].astype(F32)
    grad_one = res[3 * C :].astype(F32)
    return (features[None], small[:10], small[10], small[11], grad_one, grad_two)


def solution(mesh):
    return jax.shard_map(
        functools.partial(shards, mesh.shape["tm"], mesh.shape["rec"]),
        mesh=mesh,
        in_specs=(P("rec", "tm"), P(), P(), P(), P(), P(), P("rec", "tm", None)),
        out_specs=(P("rec", "tm", None), P(), P(), P(), P(), P()),
        check_vma=False,
    )
```
